32 devices in a mesh: section: 2 (over core), dp: 16 (over z, y, x).
Axes of the slice: x: 2, y: 2, z: 4, core: 2. Of those that a mesh axis runs over, the one named last changes fastest.
Arguments:
- inputs: bfloat16 [2, 32, 1024, 512], P('section', 'dp'), may hold values from -6 to 6
- lengths: int32 [2, 32], P('section', 'dp'), may hold values from 512 to 1024, as said below
- cotangent: bfloat16 [32, 1024, 512], P('dp'), may hold values from -6 to 6
- qkv_weight: bfloat16 [2, 512, 1536], P('section'), may hold values from -0.25 to 0.25
- out_weight: bfloat16 [2, 512, 512], P('section'), may hold values from -4 to 4
- cross_weight: bfloat16 [2, 512, 1024], P('section'), may hold values from -2.1283914 to 2.1283914
- ffn_in: bfloat16 [2, 512, 2048], P('section'), may hold values from -0.25 to 0.25
- ffn_out: bfloat16 [2, 2048, 512], P('section'), may hold values from -0.125 to 0.125
- norm_gain: float32 [2, 2, 512], P('section'), may hold values from 0.5 to 1.5
- norm_bias: float32 [2, 2, 512], P('section'), may hold values from -1.5 to 1.5
- cross_norm: float32 [2, 512], replicated, may hold values from -1.5 to 1.5
Outputs:
- layer_out: float32 [2, 32, 1024, 512], P('section', 'dp')
- input_grad: float32 [2, 32, 1024, 512], P('section', 'dp')
- qkv_grad: float32 [2, 512, 1536], P('section')
- out_grad: float32 [2, 512, 512], P('section')
- cross_grad: float32 [2, 512, 1024], P('section')
- ffn_in_grad: float32 [2, 512, 2048], P('section')
- ffn_out_grad: float32 [2, 2048, 512], P('section')
- gain_grad: float32 [2, 2, 512], P('section')
- bias_grad: float32 [2, 2, 512], P('section')
- cross_norm_grad: float32 [2, 512], P('section')
The draws below stay inside these ranges and needn't reach their ends.
Inputs may be any that keep to these rules, and one draw needn't show every extreme that they name: `lengths`: the live slots of a sequence come first. In each of the two rows one sequence fills all 1024 slots.
All inputs are finite; a program needn't handle non-finite values.
Results may differ from the reference program's by a relative error of at most 0.018.
Values may be sent and summed in bfloat16 or wider, within the bound.
No kernel may reach another device: no remote copies, remote signals or barrier semaphores. Data moves between devices by JAX's collectives and lax.ppermute only.
A program may use at most 256 MiB of HBM per device.

```python
import math
import jax
import jax.numpy as jnp
from jax import lax

D = 512
HEADS = 8
HEAD_DIM = 64
FF = 2048
SEQ_LEN = 1024
NSEQ = 32


def draw_lengths(key, part):
    key = jax.random.fold_in(key, 11)
    base_key, pick_key = jax.random.split(key)
    drawn = jax.random.randint(base_key, (2, NSEQ), SEQ_LEN // 2, SEQ_LEN + 1, dtype=jnp.int32)
    chosen = jax.random.randint(pick_key, (2, 1), 0, NSEQ, dtype=jnp.int32)
    column = lax.broadcasted_iota(jnp.int32, (2, NSEQ), 1)
    return jnp.where(column == chosen, SEQ_LEN, drawn).astype(jnp.int32)


def draw_cross_weight(key, part):
    key = jax.random.fold_in(key, 23)
    shape_all = (2, D, 2 * D)
    base = jnp.clip(jax.random.normal(key, shape_all, jnp.float32), -3.0, 3.0)
    section_pos = lax.broadcasted_iota(jnp.int32, shape_all, 0)
    column = lax.broadcasted_iota(jnp.int32, shape_all, 2)
    boost = math.sqrt(D / max(4 * D // SEQ_LEN, 1))
    factor = jnp.where(jnp.logical_and(section_pos == 1, column >= D), boost, 1.0)
    return (base * factor * (1.0 / math.sqrt(D))).astype(jnp.bfloat16)


def draw_cross_norm(key, part):
    key = jax.random.fold_in(key, 37)
    noise = jnp.clip(jax.random.normal(key, (2, D), jnp.float32), -5.0, 5.0)
    row_pos = lax.broadcasted_iota(jnp.int32, (2, D), 0)
    return jnp.where(row_pos == 0, 1.0 + 0.1 * noise, 0.3 * noise).astype(jnp.float32)


def steps_of(key, shape, pieces, smallest, high):
    loudness, own = 1.0, jax.random.fold_in(key, 6)
    for axis_at, shards_of in pieces:
        steps = jnp.exp(jax.random.uniform(jax.random.fold_in(own, axis_at), (shards_of,), jnp.float32, smallest / len(pieces), high / len(pieces)))
        loudness = loudness * jnp.repeat(steps, shape[axis_at] // shards_of).reshape([-1 if axis == axis_at else 1 for axis in range(len(shape))])
    return loudness


def scatter_about(own_key, extent, deviation, bound, pieces=(), kind=jnp.bfloat16):
    values = jax.random.normal(own_key, extent, jnp.float32) * deviation
    if len(pieces) > 0:
        values = steps_of(own_key, extent, pieces, -0.22, 0.18) * values
    return jnp.clip(values, min=-bound, max=bound).astype(kind)


def setup_inputs(seed: int = 0) -> dict:
    streams_of = jax.random.split(jax.random.key(seed), 12)
    inputs = scatter_about(streams_of[0], (2, NSEQ, SEQ_LEN, D), 1.0, 6.0, ((0, 2), (1, 16)))
    lengths = draw_lengths(jax.random.fold_in(streams_of[11], 71), 0)
    cotangent = scatter_about(streams_of[2], (NSEQ, SEQ_LEN, D), 1.0, 6.0, ((0, 16),))
    qkv_weight = scatter_about(streams_of[3], (2, D, 3 * D), D ** -0.5, 0.25, ((0, 2),))
    out_weight = scatter_about(streams_of[4], (2, D, D), (max(4 * D // SEQ_LEN, 1)) ** -0.5, 4.0, ((0, 2),))
    cross_weight = draw_cross_weight(jax.random.fold_in(streams_of[11], 71), 0)
    ffn_in = scatter_about(streams_of[6], (2, D, FF), D ** -0.5, 0.25, ((0, 2),))
    ffn_out = scatter_about(streams_of[7], (2, FF, D), FF ** -0.5, 0.125, ((0, 2),))
    norm_gain = jnp.clip(1.0 + 0.1 * jax.random.normal(streams_of[8], (2, 2, D), jnp.float32), 0.5, 1.5)
    norm_bias = scatter_about(streams_of[9], (2, 2, D), 0.3, 1.5, ((0, 2),), jnp.float32)
    cross_norm = draw_cross_norm(jax.random.fold_in(streams_of[11], 71), 0)
    return dict(inputs=inputs, lengths=lengths, cotangent=cotangent, qkv_weight=qkv_weight, out_weight=out_weight, cross_weight=cross_weight, ffn_in=ffn_in, ffn_out=ffn_out, norm_gain=norm_gain, norm_bias=norm_bias, cross_norm=cross_norm)


@jax.custom_vjp
def low(v):
    return lax.optimization_barrier(v.astype(jnp.bfloat16)).astype(jnp.float32)

@jax.custom_vjp
def low_back(v):
    return v

def low_keep(v):
    return (low(v), None)

def low_pass(kept, grad):
    return (grad,)

def back_keep(v):
    return (v, None)

def back_low(kept, grad):
    return (low(grad),)
low.defvjp(low_keep, low_pass)
low_back.defvjp(back_keep, back_low)

def product(left_side, right_side):
    return jnp.dot(left_side, right_side, precision=lax.Precision.HIGHEST)

def layer_norm(field_in, gain_row, bias_row):
    centred = field_in - lax.optimization_barrier(jnp.mean(field_in, -1, keepdims=True))
    spread = lax.optimization_barrier(jnp.mean(centred * centred, -1, keepdims=True))
    return centred * lax.rsqrt(spread + 1e-05) * gain_row + bias_row

def attention(queries, key_rows, value_rows, key_limit, causal):
    total_rows = queries.shape[0]
    block_rows = min(512, total_rows)
    score_scale = 1.0 / math.sqrt(HEAD_DIM)
    query_blocks = queries.reshape(total_rows // block_rows, block_rows, HEADS, HEAD_DIM)
    key_heads = key_rows.reshape(-1, HEADS, HEAD_DIM)
    value_heads = value_rows.reshape(-1, HEADS, HEAD_DIM)
    starts = jnp.arange(total_rows // block_rows, dtype=jnp.int32) * block_rows

    def one_block(packed):
        query_part, start_row = packed
        raw_scores = jnp.einsum('qhd,khd->hqk', query_part, key_heads, precision=lax.Precision.HIGHEST)
        scores = low_back(raw_scores) * score_scale
        shape_pair = (block_rows, key_heads.shape[0])
        key_pos = lax.broadcasted_iota(jnp.int32, shape_pair, 1)
        allowed = key_pos < key_limit
        if causal:
            query_pos = start_row + lax.broadcasted_iota(jnp.int32, shape_pair, 0)
            allowed = jnp.logical_and(allowed, key_pos <= query_pos)
        scores = jnp.where(allowed[None], scores, -1e+30)
        prob_rows = low(jax.nn.softmax(scores, axis=-1))
        return jnp.einsum('hqk,khd->qhd', prob_rows, value_heads, precision=lax.Precision.HIGHEST)
    blocks_out = lax.map(jax.checkpoint(one_block), (query_blocks, starts))
    return blocks_out.reshape(total_rows, HEADS * HEAD_DIM)

def self_block(source, packed_weight, out_weight, key_limit, causal):
    packed = low(low_back(product(low(source), packed_weight)))
    attended = attention(packed[:, :D], packed[:, D:2 * D], packed[:, 2 * D:], key_limit, causal)
    return low_back(product(low(low_back(attended)), out_weight))

def feed_forward(hidden, in_weight, down_weight):
    raised = low_back(product(low(hidden), in_weight))
    return low_back(product(low(jax.nn.gelu(raised, approximate=False)), down_weight))

def encoder(source, source_limit, params):
    packed_weight, out_weight, cross_weight, in_weight, down_weight, gains, biases = params
    hidden = layer_norm(source + self_block(source, packed_weight, out_weight, source_limit, False), gains[0], biases[0])
    result = layer_norm(hidden + feed_forward(hidden, in_weight, down_weight) + source, gains[1], biases[1])
    memory = low(low_back(product(low(result), cross_weight)))
    return (result, memory)

def decoder(target, target_limit, memory, source_limit, params, cross_norm):
    packed_weight, out_weight, cross_weight, in_weight, down_weight, gains, biases = params
    hidden = layer_norm(target + self_block(target, packed_weight, out_weight, target_limit, True), gains[0], biases[0])
    asked = low(low_back(product(low(hidden), cross_weight[:, :D])))
    context = attention(asked, memory[:, :D], memory[:, D:], source_limit, False)
    exit_rows = low_back(product(low(low_back(context)), cross_weight[:, D:]))
    mixed = layer_norm(hidden + exit_rows, cross_norm[0], cross_norm[1])
    return layer_norm(mixed + feed_forward(mixed, in_weight, down_weight) + target, gains[1], biases[1])

def forward_all(inputs, lengths, qkv_weight, out_weight, cross_weight, ffn_in, ffn_out, norm_gain, norm_bias, cross_norm):
    enc_params = (qkv_weight[0], out_weight[0], cross_weight[0], ffn_in[0], ffn_out[0], norm_gain[0], norm_bias[0])
    dec_params = (qkv_weight[1], out_weight[1], cross_weight[1], ffn_in[1], ffn_out[1], norm_gain[1], norm_bias[1])

    def one_pair(running, packed):
        source, target, source_limit, target_limit = packed
        enc_rows, memory = encoder(source, source_limit, enc_params)
        dec_rows = decoder(target, target_limit, memory, source_limit, dec_params, cross_norm)
        return (running, (enc_rows, dec_rows))
    start_carry = jnp.zeros((), jnp.float32)
    _, (enc_all, dec_all) = lax.scan(jax.checkpoint(one_pair), start_carry, (inputs[0], inputs[1], lengths[0], lengths[1]))
    return jnp.stack([enc_all, dec_all])

def reference(inputs, lengths, cotangent, qkv_weight, out_weight, cross_weight, ffn_in, ffn_out, norm_gain, norm_bias, cross_norm):

    def wrapped(inputs_wide, qkv_wide, out_wide, cross_wide, in_wide, down_wide, gain_wide, bias_wide, cross_wide_norm):
        return forward_all(inputs_wide, lengths, qkv_wide, out_wide, cross_wide, in_wide, down_wide, gain_wide, bias_wide, cross_wide_norm)
    layer_out, pullback = jax.vjp(wrapped, inputs.astype(jnp.float32), qkv_weight.astype(jnp.float32), out_weight.astype(jnp.float32), cross_weight.astype(jnp.float32), ffn_in.astype(jnp.float32), ffn_out.astype(jnp.float32), norm_gain.astype(jnp.float32), norm_bias.astype(jnp.float32), cross_norm.astype(jnp.float32))
    seed_wide = cotangent.astype(jnp.float32)
    seed_all = jnp.stack([jnp.zeros_like(seed_wide), seed_wide])
    grads = pullback(seed_all)
    return (layer_out, grads[0], grads[1], grads[2], grads[3], grads[4], grads[5], grads[6], grads[7], grads[8])
```

```python
from functools import partial
import math

import jax
import jax.numpy as jnp
from jax import lax
from jax.experimental import pallas as pl
from jax.experimental.pallas import tpu as pltpu
from jax.sharding import PartitionSpec as P

F32, BF16 = jnp.float32, jnp.bfloat16
HEAD_DIM = 64
PAIR = 2 * HEAD_DIM
LOG2E = math.log2(math.e)
NEG = -1e30
EPS = 1e-05
SCALE = 1.0 / math.sqrt(HEAD_DIM)
VMEM_LIMIT = 56 << 20


def nn(left, right):
    return lax.dot_general(left, right, (((1,), (0,)), ((), ())), preferred_element_type=F32)


def nt(left, right):
    return lax.dot_general(left, right, (((1,), (1,)), ((), ())), preferred_element_type=F32)


def tn(left, right):
    return lax.dot_general(left, right, (((0,), (0,)), ((), ())), preferred_element_type=F32)


def lanes(shape):
    return lax.broadcasted_iota(jnp.int32, shape, 1)


def rows_of(shape):
    return lax.broadcasted_iota(jnp.int32, shape, 0)


def norm_forward(field, gain, bias):
    centred = field - jnp.mean(field, -1, keepdims=True)
    inverse = lax.rsqrt(jnp.mean(centred * centred, -1, keepdims=True) + EPS)
    normed = centred * inverse
    return normed * gain + bias, normed, inverse


def norm_backward(grad, normed, inverse, gain):
    scaled = grad * gain
    inner = (
        scaled
        - jnp.mean(scaled, -1, keepdims=True)
        - normed * jnp.mean(scaled * normed, -1, keepdims=True)
    )
    gain_grad = jnp.sum(grad * normed, 0, keepdims=True)
    return inner * inverse, gain_grad, jnp.sum(grad, 0, keepdims=True)


def gelu_parts(raised):
    cumulative = 0.5 * (1.0 + lax.erf(raised * (1.0 / math.sqrt(2.0))))
    density = jnp.exp(-0.5 * raised * raised) * (1.0 / math.sqrt(2.0 * math.pi))
    return raised * cumulative, cumulative + raised * density


def split3(value):
    high = value.astype(BF16)
    rest = value - high.astype(F32)
    middle = rest.astype(BF16)
    return high, middle, (rest - middle.astype(F32)).astype(BF16)


def attend_body(limit, q_ref, k_ref, v_ref, o_ref, l_ref, ke, ve, causal, block):
    total = q_ref.shape[0]
    lane = lanes((total, PAIR))
    ke[:, :PAIR] = k_ref[...]
    ke[:, PAIR:] = jnp.where((lane == 3) & (rows_of((total, PAIR)) >= limit), NEG, 0.0).astype(BF16)
    ve[:, :PAIR] = v_ref[...]
    ve[:, PAIR:] = jnp.ones((total, PAIR), BF16)
    lane_q = lanes((block, PAIR))
    first = lane_q < HEAD_DIM
    aux = jnp.where(lane_q == 3, 1.0, 0.0).astype(BF16)
    for j in range(total // block):
        here = pl.ds(j * block, block)
        seen = (j + 1) * block if causal else total
        q_pair = q_ref[here, :]
        zero = jnp.zeros_like(q_pair)
        parts = []
        for h in range(2):
            own = first if h == 0 else jnp.logical_not(first)
            q_ext = jnp.concatenate([jnp.where(own, q_pair, zero), aux], 1)
            scores = nt(q_ext, ke[:seen, :])
            if causal:
                keep = lanes((block, block)) <= rows_of((block, block))
                edge = jnp.where(keep, scores[:, j * block :], NEG)
                scores = jnp.concatenate([scores[:, : j * block], edge], 1) if j else edge
            peak = jnp.max(scores, -1, keepdims=True)
            probs = jnp.exp2(scores - peak).astype(BF16)
            mixed = nn(probs, ve[:seen, :])
            sums = mixed[:, PAIR:]
            parts.append((mixed[:, :PAIR] / sums, peak + jnp.log2(sums)))
        o_ref[here, :] = jnp.where(first, parts[0][0], parts[1][0]).astype(BF16)
        l_ref[here, :] = jnp.where(first, parts[0][1], parts[1][1])


def attend_back_body(limit, q_ref, k_ref, v_ref, o_ref, l_ref, g_ref, scr, causal, block):
    ke, ve, dka, dva, dqa = scr
    total = q_ref.shape[0]
    lane = lanes((total, PAIR)) % HEAD_DIM
    ones = jnp.where(lane < 3, 1.0, 0.0)
    ke[:, :PAIR] = k_ref[...]
    outside = (lane == 3) & (rows_of((total, PAIR)) >= limit)
    ke[:, PAIR:] = jnp.where(outside, NEG, ones).astype(BF16)
    ve[:, :PAIR] = v_ref[...]
    ve[:, PAIR:] = ones.astype(BF16)
    lane_q = lanes((block, PAIR))
    first = lane_q < HEAD_DIM
    spot = lane_q % HEAD_DIM
    unit = jnp.where(spot == 3, 1.0, 0.0).astype(BF16)
    for j in range(total // block):
        here = pl.ds(j * block, block)
        low = j * block
        seen = low + block if causal else total
        q_pair = q_ref[here, :]
        g_pair = g_ref[here, :]
        zero = jnp.zeros_like(q_pair)
        product = g_pair.astype(F32) * o_ref[here, :].astype(F32)
        a, b, c = split3(-l_ref[here, :])
        aux_q = jnp.where(spot == 0, a, jnp.where(spot == 1, b, jnp.where(spot == 2, c, unit)))
        dqs = []
        for h in range(2):
            own = first if h == 0 else jnp.logical_not(first)
            inner = jnp.sum(jnp.where(own, product, 0.0), -1, keepdims=True)
            a, b, c = split3(jnp.broadcast_to(-inner, (block, PAIR)))
            aux_g = jnp.where(spot == 0, a, jnp.where(spot == 1, b, jnp.where(spot == 2, c, zero)))
            q_own = jnp.where(own, q_pair, zero)
            g_own = jnp.where(own, g_pair, zero)
            q_ext = jnp.concatenate([q_own, jnp.where(own, aux_q, zero)], 1)
            g_ext = jnp.concatenate([g_own, jnp.where(own, aux_g, zero)], 1)
            probs = jnp.exp2(nt(ke[:seen, :], q_ext))
            if causal:
                keep = rows_of((block, block)) <= lanes((block, block))
                edge = jnp.where(keep, probs[low:, :], 0.0)
                probs = jnp.concatenate([probs[:low, :], edge], 0) if j else edge
            slope = (probs * nt(ve[:seen, :], g_ext)).astype(BF16)
            dv = nn(probs.astype(BF16), g_own)
            dk = nn(slope, q_own)
            if h == 0 and causal:
                if j:
                    dva[:low, :] += dv[:low]
                    dka[:low, :] += dk[:low]
                dva[low:seen, :] = dv[low:]
                dka[low:seen, :] = dk[low:]
            elif h == 0 and j == 0:
                dva[...] = dv
                dka[...] = dk
            else:
                dva[:seen, :] += dv
                dka[:seen, :] += dk
            dqs.append(jnp.transpose(tn(k_ref[:seen, :], slope)))
        dqa[here, :] = (jnp.where(first, dqs[0], dqs[1]) * SCALE).astype(BF16)


def attend_scratch(total):
    return [
        pltpu.VMEM((total, 2 * PAIR), BF16),
        pltpu.VMEM((total, 2 * PAIR), BF16),
        pltpu.VMEM((total, PAIR), F32),
        pltpu.VMEM((total, PAIR), F32),
        pltpu.VMEM((total, PAIR), BF16),
    ]


def params(**extra):
    return pltpu.CompilerParams(vmem_limit_bytes=VMEM_LIMIT, **extra)


def smem():
    return pl.BlockSpec(memory_space=pltpu.SMEM)


def whole(array):
    zeros = (0,) * array.ndim
    return pl.BlockSpec(array.shape, lambda *_: zeros, pipeline_mode=pl.Buffered(1))


def column(total, shift=0):
    return pl.BlockSpec((total, PAIR), lambda p: (0, p + shift))


def self_forward(rows, weight, limit, causal):
    total, width = rows.shape
    pairs = width // PAIR
    block = min(256, total)

    def kernel(lim, x_ref, wq, wk, wv, q_ref, k_ref, v_ref, o_ref, l_ref, ke, ve):
        rows_in = x_ref[...]
        q_ref[...] = (nn(rows_in, wq[...]) * (SCALE * LOG2E)).astype(BF16)
        k_ref[...] = nn(rows_in, wk[...]).astype(BF16)
        v_ref[...] = nn(rows_in, wv[...]).astype(BF16)
        attend_body(lim[0], q_ref, k_ref, v_ref, o_ref, l_ref, ke, ve, causal, block)

    return pl.pallas_call(
        kernel,
        grid=(pairs,),
        in_specs=[smem(), whole(rows)] + [column(width, s * pairs) for s in range(3)],
        out_specs=[column(total)] * 5,
        out_shape=[jax.ShapeDtypeStruct((total, width), BF16)] * 4
        + [jax.ShapeDtypeStruct((total, width), F32)],
        scratch_shapes=attend_scratch(total)[:2],
        compiler_params=params(),
    )(limit, rows, weight, weight, weight)


def cross_forward(asked, memory, limit):
    total, width = asked.shape
    pairs = width // PAIR
    block = min(256, total)

    def kernel(lim, q_ref, k_ref, v_ref, o_ref, l_ref, ke, ve):
        attend_body(lim[0], q_ref, k_ref, v_ref, o_ref, l_ref, ke, ve, False, block)

    return pl.pallas_call(
        kernel,
        grid=(pairs,),
        in_specs=[smem(), column(total), column(total), column(total, pairs)],
        out_specs=[column(total)] * 2,
        out_shape=[
            jax.ShapeDtypeStruct((total, width), BF16),
            jax.ShapeDtypeStruct((total, width), F32),
        ],
        scratch_shapes=attend_scratch(total)[:2],
        compiler_params=params(),
    )(limit, asked, memory, memory)


def cross_backward(asked, memory, limit, context, logs, grad):
    total, width = asked.shape
    pairs = width // PAIR
    block = min(256, total)

    def kernel(lim, q_ref, k_ref, v_ref, o_ref, l_ref, g_ref, dq_ref, dk_ref, dv_ref, *scr):
        attend_back_body(lim[0], q_ref, k_ref, v_ref, o_ref, l_ref, g_ref, scr, False, block)
        dq_ref[...] = scr[4][...]
        dk_ref[...] = (scr[2][...] * (1.0 / LOG2E)).astype(BF16)
        dv_ref[...] = scr[3][...].astype(BF16)

    return pl.pallas_call(
        kernel,
        grid=(pairs,),
        in_specs=[smem(), column(total), column(total), column(total, pairs)] + [column(total)] * 3,
        out_specs=[column(total)] * 3,
        out_shape=[jax.ShapeDtypeStruct((total, width), BF16)] * 3,
        scratch_shapes=attend_scratch(total),
        compiler_params=params(),
    )(limit, asked, memory, memory, context, logs, grad)


def self_backward(rows, weight, limit, stored, grad, residual, causal):
    total, width = rows.shape
    pairs = width // PAIR
    block = min(256, total)
    queries, keys, values, attended, logs = stored

    def kernel(
        lim, x_ref, wq, wk, wv, q_ref, k_ref, v_ref, o_ref, l_ref, g_ref, r_ref,
        dx_ref, gq_ref, gk_ref, gv_ref, dxa, *scr,
    ):
        step = pl.program_id(0)
        attend_back_body(lim[0], q_ref, k_ref, v_ref, o_ref, l_ref, g_ref, scr, causal, block)
        dq = scr[4][...]
        dk = (scr[2][...] * (1.0 / LOG2E)).astype(BF16)
        dv = scr[3][...].astype(BF16)
        rows_in = x_ref[...]
        gq_ref[...] = tn(rows_in, dq).astype(BF16)
        gk_ref[...] = tn(rows_in, dk).astype(BF16)
        gv_ref[...] = tn(rows_in, dv).astype(BF16)
        packed = jnp.concatenate([dq, dk, dv], 1)
        weights = jnp.concatenate([wq[...], wk[...], wv[...]], 1)
        back = nt(packed, weights)

        @pl.when(step == 0)
        def _():
            dxa[...] = r_ref[...] + back

        @pl.when(step > 0)
        def _():
            dxa[...] += back

        @pl.when(step == pairs - 1)
        def _():
            dx_ref[...] = dxa[...]

    return pl.pallas_call(
        kernel,
        grid=(pairs,),
        in_specs=[smem(), whole(rows)]
        + [column(width, s * pairs) for s in range(3)]
        + [column(total)] * 6
        + [whole(residual)],
        out_specs=[whole(residual)] + [column(width)] * 3,
        out_shape=[jax.ShapeDtypeStruct((total, width), F32)]
        + [jax.ShapeDtypeStruct((width, width), BF16)] * 3,
        scratch_shapes=[pltpu.VMEM((total, width), F32)] + attend_scratch(total),
        compiler_params=params(),
    )(
        limit, rows, weight, weight, weight, queries, keys, values, attended, logs, grad, residual
    )


def row_block(block, width, last=None):
    if last is None:
        return pl.BlockSpec((block, width), lambda i: (i, 0))
    return pl.BlockSpec((block, width), lambda i: (jnp.minimum(i, last), 0))


def encoder_middle(attended, rows, weights, norms):
    out_weight, cross_weight, in_weight, down_weight = weights
    total, width = rows.shape
    hidden = in_weight.shape[1]
    block = min(256, total)

    def kernel(
        o_ref, x_ref, wo, wc, wi, wd, nr,
        y_ref, m_ref, n1_ref, r1_ref, n2_ref, r2_ref, f_ref, s_ref,
    ):
        source = x_ref[...].astype(F32)
        first, n1, r1 = norm_forward(source + nn(o_ref[...], wo[...]), nr[0:1, :], nr[2:3, :])
        active, slope = gelu_parts(nn(first.astype(BF16), wi[...]))
        active = active.astype(BF16)
        last, n2, r2 = norm_forward(first + nn(active, wd[...]) + source, nr[1:2, :], nr[3:4, :])
        y_ref[...] = last
        m_ref[...] = nn(last.astype(BF16), wc[...]).astype(BF16)
        n1_ref[...] = n1
        n2_ref[...] = n2
        r1_ref[...] = jnp.broadcast_to(r1, r1_ref.shape)
        r2_ref[...] = jnp.broadcast_to(r2, r2_ref.shape)
        f_ref[...] = active
        s_ref[...] = slope.astype(BF16)

    shapes = [
        (width, F32), (2 * width, BF16), (width, F32), (128, F32),
        (width, F32), (128, F32), (hidden, BF16), (hidden, BF16),
    ]
    return pl.pallas_call(
        kernel,
        grid=(total // block,),
        in_specs=[row_block(block, width)] * 2
        + [whole(a) for a in (out_weight, cross_weight, in_weight, down_weight, norms)],
        out_specs=[row_block(block, w) for w, _ in shapes],
        out_shape=[jax.ShapeDtypeStruct((total, w), d) for w, d in shapes],
        compiler_params=params(),
    )(attended, rows, out_weight, cross_weight, in_weight, down_weight, norms)


def decoder_middle(attended, rows, out_weight, cross_weight, norms):
    total, width = rows.shape
    block = min(256, total)

    def kernel(o_ref, x_ref, wo, wc, nr, q_ref, n1_ref, r1_ref):
        target = x_ref[...].astype(F32)
        first, n1, r1 = norm_forward(target + nn(o_ref[...], wo[...]), nr[0:1, :], nr[2:3, :])
        asked = nn(first.astype(BF16), wc[...])
        q_ref[...] = (asked * (SCALE * LOG2E)).astype(BF16)
        n1_ref[...] = n1
        r1_ref[...] = jnp.broadcast_to(r1, r1_ref.shape)

    half = pl.BlockSpec((width, width), lambda i: (0, 0), pipeline_mode=pl.Buffered(1))
    shapes = [(width, BF16), (width, F32), (128, F32)]
    return pl.pallas_call(
        kernel,
        grid=(total // block,),
        in_specs=[row_block(block, width)] * 2 + [whole(out_weight), half, whole(norms)],
        out_specs=[row_block(block, w) for w, _ in shapes],
        out_shape=[jax.ShapeDtypeStruct((total, w), d) for w, d in shapes],
        compiler_params=params(),
    )(attended, rows, out_weight, cross_weight, norms)


def add_rows(ref, step, grads):
    @pl.when(step == 0)
    def _():
        ref[...] = jnp.zeros_like(ref)

    for at, grad in enumerate(grads):
        ref[at : at + 1, :] += grad


def decoder_tail(context, n1, rows, seeds, weights, norms):
    cross_weight, in_weight, down_weight = weights
    total, width = rows.shape
    hidden = in_weight.shape[1]
    block = min(256, total)
    steps = total // block
    tiles = hidden // width

    def kernel(
        c_ref, n1_ref, x_ref, g_ref, wc, wi, wd, nr,
        y_ref, dl_ref, dm_ref, dc_ref, gi_ref, gd_ref, gc_ref, gn_ref,
        mixed_all, raised_all, active_all, down_all, mid_all, con_all,
    ):
        step = pl.program_id(0)

        @pl.when(step < steps)
        def _():
            here = pl.ds(pl.multiple_of(step * block, block), block)
            target = x_ref[...].astype(F32)
            first = n1_ref[...] * nr[0:1, :] + nr[2:3, :]
            mixed, nm, rm = norm_forward(first + nn(c_ref[...], wc[...]), nr[4:5, :], nr[5:6, :])
            mixed_low = mixed.astype(BF16)
            active, slope = gelu_parts(nn(mixed_low, wi[...]))
            active = active.astype(BF16)
            last, n2, r2 = norm_forward(mixed + nn(active, wd[...]) + target, nr[1:2, :], nr[3:4, :])
            y_ref[...] = last
            dlast, gain2, bias2 = norm_backward(g_ref[...].astype(F32), n2, r2, nr[1:2, :])
            down = dlast.astype(BF16)
            raised = (nt(down, wd[...]) * slope).astype(BF16)
            dmixed = dlast + nt(raised, wi[...])
            dmid, gainm, biasm = norm_backward(dmixed, nm, rm, nr[4:5, :])
            mid = dmid.astype(BF16)
            dl_ref[...] = dlast
            dm_ref[...] = dmid
            dc_ref[...] = nt(mid, wc[...]).astype(BF16)
            mixed_all[here, :] = mixed_low
            raised_all[here, :] = raised
            active_all[here, :] = active
            down_all[here, :] = down
            mid_all[here, :] = mid
            con_all[here, :] = c_ref[...]
            add_rows(gn_ref, step, (gain2, bias2, gainm, biasm))

        @pl.when(step >= steps)
        def _():
            tile = step - steps
            here = pl.ds(pl.multiple_of(tile * width, width), width)
            gi_ref[...] = tn(mixed_all[...], raised_all[:, here]).astype(BF16)
            gd_ref[...] = tn(active_all[:, here], down_all[...]).astype(BF16)

        @pl.when(step == steps)
        def _():
            gc_ref[...] = tn(con_all[...], mid_all[...]).astype(BF16)

    last_row = steps - 1
    half = pl.BlockSpec((width, width), lambda i: (0, 1), pipeline_mode=pl.Buffered(1))
    tile_at = lambda i: jnp.maximum(i - steps, 0)
    return pl.pallas_call(
        kernel,
        grid=(steps + tiles,),
        in_specs=[row_block(block, width, last_row)] * 4
        + [half, whole(in_weight), whole(down_weight), whole(norms)],
        out_specs=[row_block(block, width, last_row)] * 4
        + [
            pl.BlockSpec((width, width), lambda i: (0, tile_at(i))),
            pl.BlockSpec((width, width), lambda i: (tile_at(i), 0)),
            pl.BlockSpec((width, width), lambda i: (0, 0)),
            pl.BlockSpec((8, width), lambda i: (0, 0)),
        ],
        out_shape=[
            jax.ShapeDtypeStruct((total, width), F32),
            jax.ShapeDtypeStruct((total, width), F32),
            jax.ShapeDtypeStruct((total, width), F32),
            jax.ShapeDtypeStruct((total, width), BF16),
            jax.ShapeDtypeStruct((width, hidden), BF16),
            jax.ShapeDtypeStruct((hidden, width), BF16),
            jax.ShapeDtypeStruct((width, width), BF16),
            jax.ShapeDtypeStruct((8, width), F32),
        ],
        scratch_shapes=[
            pltpu.VMEM((total, width), BF16),
            pltpu.VMEM((total, hidden), BF16),
            pltpu.VMEM((total, hidden), BF16),
            pltpu.VMEM((total, width), BF16),
            pltpu.VMEM((total, width), BF16),
            pltpu.VMEM((total, width), BF16),
        ],
        compiler_params=params(),
    )(context, n1, rows, seeds, cross_weight, in_weight, down_weight, norms)


def encoder_back(dkeys, dvalues, attended, kept, weights, norms):
    out_weight, cross_weight, in_weight, down_weight = weights
    n1, r1, n2, r2, active, slope = kept
    total, width = n1.shape
    hidden = in_weight.shape[1]
    block = min(256, total)
    steps = total // block
    tiles = hidden // width

    def kernel(
        dk_ref, dv_ref, o_ref, n1_ref, r1_ref, n2_ref, r2_ref, f_ref, s_ref, wo, wc, wi, wd, nr,
        da_ref, res_ref, gi_ref, gd_ref, gc_ref, go_ref, gn_ref,
        hid_all, raised_all, active_all, down_all, first_all, att_all, last_all, dk_all, dv_all,
    ):
        step = pl.program_id(0)

        @pl.when(step < steps)
        def _():
            here = pl.ds(pl.multiple_of(step * block, block), block)
            dk, dv = dk_ref[...], dv_ref[...]
            n1_rows, n2_rows = n1_ref[...], n2_ref[...]
            dy = nt(dk, wc[:, :width]) + nt(dv, wc[:, width:])
            dlast, gain2, bias2 = norm_backward(dy, n2_rows, r2_ref[:, 0:1], nr[1:2, :])
            down = dlast.astype(BF16)
            raised = (nt(down, wd[...]) * s_ref[...].astype(F32)).astype(BF16)
            dhidden = dlast + nt(raised, wi[...])
            dfirst, gain1, bias1 = norm_backward(dhidden, n1_rows, r1_ref[:, 0:1], nr[0:1, :])
            first = dfirst.astype(BF16)
            da_ref[...] = nt(first, wo[...]).astype(BF16)
            res_ref[...] = dlast + dfirst
            hid_all[here, :] = (n1_rows * nr[0:1, :] + nr[2:3, :]).astype(BF16)
            last_all[here, :] = (n2_rows * nr[1:2, :] + nr[3:4, :]).astype(BF16)
            raised_all[here, :] = raised
            active_all[here, :] = f_ref[...]
            down_all[here, :] = down
            first_all[here, :] = first
            att_all[here, :] = o_ref[...]
            dk_all[here, :] = dk
            dv_all[here, :] = dv
            add_rows(gn_ref, step, (gain1, gain2, bias1, bias2))

        @pl.when(step >= steps)
        def _():
            tile = step - steps
            here = pl.ds(pl.multiple_of(tile * width, width), width)
            gi_ref[...] = tn(hid_all[...], raised_all[:, here]).astype(BF16)
            gd_ref[...] = tn(active_all[:, here], down_all[...]).astype(BF16)

        @pl.when(step == steps)
        def _():
            gc_ref[:, :width] = tn(last_all[...], dk_all[...]).astype(BF16)
            gc_ref[:, width:] = tn(last_all[...], dv_all[...]).astype(BF16)
            go_ref[...] = tn(att_all[...], first_all[...]).astype(BF16)

    last_row = steps - 1
    row = row_block(block, width, last_row)
    thin = row_block(block, 128, last_row)
    wide = row_block(block, hidden, last_row)
    tile_at = lambda i: jnp.maximum(i - steps, 0)
    return pl.pallas_call(
        kernel,
        grid=(steps + tiles,),
        in_specs=[row] * 3
        + [row, thin, row, thin, wide, wide]
        + [whole(a) for a in (out_weight, cross_weight, in_weight, down_weight, norms)],
        out_specs=[row] * 2
        + [
            pl.BlockSpec((width, width), lambda i: (0, tile_at(i))),
            pl.BlockSpec((width, width), lambda i: (tile_at(i), 0)),
            pl.BlockSpec((width, 2 * width), lambda i: (0, 0)),
            pl.BlockSpec((width, width), lambda i: (0, 0)),
            pl.BlockSpec((8, width), lambda i: (0, 0)),
        ],
        out_shape=[
            jax.ShapeDtypeStruct((total, width), BF16),
            jax.ShapeDtypeStruct((total, width), F32),
            jax.ShapeDtypeStruct((width, hidden), BF16),
            jax.ShapeDtypeStruct((hidden, width), BF16),
            jax.ShapeDtypeStruct((width, 2 * width), BF16),
            jax.ShapeDtypeStruct((width, width), BF16),
            jax.ShapeDtypeStruct((8, width), F32),
        ],
        scratch_shapes=[
            pltpu.VMEM((total, width), BF16),
            pltpu.VMEM((total, hidden), BF16),
            pltpu.VMEM((total, hidden), BF16),
        ]
        + [pltpu.VMEM((total, width), BF16)] * 6,
        compiler_params=params(),
    )(
        dkeys, dvalues, attended, n1, r1, n2, r2, active, slope,
        out_weight, cross_weight, in_weight, down_weight, norms,
    )


def decoder_back(dasked, dmid, dlast, attended, n1, r1, out_weight, cross_weight, norms):
    total, width = n1.shape
    block = min(256, total)
    steps = total // block

    def kernel(
        dq_ref, dm_ref, dl_ref, o_ref, n1_ref, r1_ref, wo, wc, nr,
        da_ref, res_ref, gc_ref, go_ref, gn_ref, hid_all, first_all, att_all, dq_all,
    ):
        step = pl.program_id(0)
        here = pl.ds(pl.multiple_of(step * block, block), block)
        dq = dq_ref[...]
        n1_rows = n1_ref[...]
        dhidden = dm_ref[...] + nt(dq, wc[...])
        dfirst, gain1, bias1 = norm_backward(dhidden, n1_rows, r1_ref[:, 0:1], nr[0:1, :])
        first = dfirst.astype(BF16)
        da_ref[...] = nt(first, wo[...]).astype(BF16)
        res_ref[...] = dl_ref[...] + dfirst
        hid_all[here, :] = (n1_rows * nr[0:1, :] + nr[2:3, :]).astype(BF16)
        first_all[here, :] = first
        att_all[here, :] = o_ref[...]
        dq_all[here, :] = dq
        add_rows(gn_ref, step, (gain1, bias1))

        @pl.when(step == steps - 1)
        def _():
            gc_ref[...] = tn(hid_all[...], dq_all[...]).astype(BF16)
            go_ref[...] = tn(att_all[...], first_all[...]).astype(BF16)

    row = row_block(block, width)
    half = pl.BlockSpec((width, width), lambda i: (0, 0), pipeline_mode=pl.Buffered(1))
    square = pl.BlockSpec((width, width), lambda i: (0, 0))
    return pl.pallas_call(
        kernel,
        grid=(steps,),
        in_specs=[row] * 5 + [row_block(block, 128), whole(out_weight), half, whole(norms)],
        out_specs=[row] * 2 + [square, square, pl.BlockSpec((8, width), lambda i: (0, 0))],
        out_shape=[
            jax.ShapeDtypeStruct((total, width), BF16),
            jax.ShapeDtypeStruct((total, width), F32),
            jax.ShapeDtypeStruct((width, width), BF16),
            jax.ShapeDtypeStruct((width, width), BF16),
            jax.ShapeDtypeStruct((8, width), F32),
        ],
        scratch_shapes=[pltpu.VMEM((total, width), BF16)] * 4,
        compiler_params=params(),
    )(dasked, dmid, dlast, attended, n1, r1, out_weight, cross_weight, norms)


def local(
    inputs,
    lengths,
    cotangent,
    qkv_weight,
    out_weight,
    cross_weight,
    ffn_in,
    ffn_out,
    norm_gain,
    norm_bias,
    cross_norm,
):
    section = lax.axis_index("section")
    first = section == 0
    swap = [(0, 1), (1, 0)]

    def swapped(value):
        return lax.ppermute(value, "section", swap)

    def pick(value, at):
        return lax.dynamic_index_in_dim(value, at, 0, keepdims=False)

    def both(own):
        other = swapped(own)
        return jnp.where(first, own, other), jnp.where(first, other, own)

    def share(value):
        own, other = pick(value, section), swapped(pick(value, 1 - section))
        return jnp.where(first, own, other), jnp.where(first, other, own)

    source, target = share(inputs[0])
    source_limit, target_limit = share(lengths[0][:, None])
    seeds = pick(cotangent, section)
    enc_qkv, dec_qkv = both(qkv_weight[0])
    enc_out, dec_out = both(out_weight[0])
    enc_cross, dec_cross = both(cross_weight[0])
    enc_in, dec_in = both(ffn_in[0])
    enc_down, dec_down = both(ffn_out[0])
    enc_norm, dec_norm = both(jnp.concatenate([norm_gain[0], norm_bias[0]], 0))
    width = source.shape[1]
    empty = jnp.zeros((2, width), F32)
    enc_norm = jnp.concatenate([enc_norm, empty, empty], 0)
    dec_norm = jnp.concatenate([dec_norm, cross_norm, empty], 0)

    enc_self = self_forward(source, enc_qkv, source_limit, False)
    dec_self = self_forward(target, dec_qkv, target_limit, True)
    enc_weights = (enc_out, enc_cross, enc_in, enc_down)
    enc_rows, memory, *enc_kept = encoder_middle(enc_self[3], source, enc_weights, enc_norm)
    asked, dec_n1, dec_r1 = decoder_middle(dec_self[3], target, dec_out, dec_cross, dec_norm)
    context, cross_logs = cross_forward(asked, memory, source_limit)
    dec_rows, dec_last, dec_mid, dcontext, dec_gi, dec_gd, dec_gco, dec_gn = decoder_tail(
        context, dec_n1, target, seeds, (dec_cross, dec_in, dec_down), dec_norm
    )
    every = ("section", "dp")
    dec_gi, dec_gd, dec_gco, dec_gn = lax.psum(
        (dec_gi, dec_gd, dec_gco, dec_gn.astype(BF16)), every
    )
    dasked, dkeys, dvalues = cross_backward(
        asked, memory, source_limit, context, cross_logs, dcontext
    )
    denc, enc_res, enc_gi, enc_gd, enc_gc, enc_go, enc_gn = encoder_back(
        dkeys, dvalues, enc_self[3], enc_kept, enc_weights, enc_norm
    )
    ddec, dec_res, dec_gcq, dec_go, dec_gn1 = decoder_back(
        dasked, dec_mid, dec_last, dec_self[3], dec_n1, dec_r1, dec_out, dec_cross, dec_norm
    )
    enc_dx, *enc_gqkv = self_backward(
        source, enc_qkv, source_limit, enc_self, denc, enc_res, False
    )
    dec_dx, *dec_gqkv = self_backward(
        target, dec_qkv, target_limit, dec_self, ddec, dec_res, True
    )
    send = tuple(
        jnp.where(first, d, e)
        for d, e in zip(
            [*dec_gqkv, dec_go, dec_gcq, dec_gn1.astype(BF16)],
            [*enc_gqkv, enc_go, enc_gc[:, :width], enc_gn.astype(BF16)],
        )
    )
    keep = tuple(
        jnp.where(first, e, d)
        for d, e in zip(
            [*dec_gqkv, dec_go, dec_gcq, dec_gn1.astype(BF16)],
            [*enc_gqkv, enc_go, enc_gc[:, :width], enc_gn.astype(BF16)],
        )
    )
    enc_gi, enc_gd, enc_gcv = lax.psum((enc_gi, enc_gd, enc_gc[:, width:]), every)
    mine = lax.psum(tuple(k + s for k, s in zip(keep, swapped(send))), "dp")

    def choose(e, d):
        return jnp.where(first, e, d).astype(F32)[None]

    def spread(e, d):
        own, other = jnp.where(first, e, d), swapped(jnp.where(first, d, e))
        low, high = jnp.where(first, own, other), jnp.where(first, other, own)
        return jnp.stack([low, high])[None]

    norm_own = mine[5].astype(F32)
    norm_dec = dec_gn.astype(F32)
    gains = jnp.where(first, norm_own[0:2], jnp.stack([norm_own[0], norm_dec[0]]))
    biases = jnp.where(first, norm_own[2:4], jnp.stack([norm_own[1], norm_dec[1]]))
    cross_row = jnp.where(first, norm_dec[2], norm_dec[3])
    return (
        spread(enc_rows, dec_rows),
        spread(enc_dx, dec_dx),
        jnp.concatenate(mine[:3], 1).astype(F32)[None],
        mine[3].astype(F32)[None],
        jnp.concatenate([mine[4], jnp.where(first, enc_gcv, dec_gco)], 1).astype(F32)[None],
        choose(enc_gi, dec_gi),
        choose(enc_gd, dec_gd),
        gains[None],
        biases[None],
        cross_row[None],
    )


def solution(mesh):
    in_specs = (
        P("section", "dp", None, None),
        P("section", "dp"),
        P("dp", None, None),
        P("section", None, None),
        P("section", None, None),
        P("section", None, None),
        P("section", None, None),
        P("section", None, None),
        P("section", None, None),
        P("section", None, None),
        P(),
    )
    out_specs = (
        P("section", "dp", None, None),
        P("section", "dp", None, None),
        P("section", None, None),
        P("section", None, None),
        P("section", None, None),
        P("section", None, None),
        P("section", None, None),
        P("section", None, None),
        P("section", None, None),
        P("section", None),
    )
    return jax.shard_map(local, mesh=mesh, in_specs=in_specs, out_specs=out_specs, check_vma=False)
```
